32 devices in a mesh: grp: 2 (over y), ctx: 8 (over z, x), ch: 2 (over core).
Axes of the slice: x: 2, y: 2, z: 4, core: 2. Of those that a mesh axis runs over, the one named last changes fastest.
Arguments:
- qkv: bfloat16 [2048, 3, 8192], P(('grp', 'ctx'), None, 'ch'), parts along dimension 0, may hold values from -6 to 6
- g_out: bfloat16 [2048, 8192], P(('grp', 'ctx'), 'ch'), parts along dimension 0, may hold values from -6 to 6
- residue: float32 [512, 16], P('ch'), may hold values from -0.26 to 0.26
- decay: float32 [512, 16], P('ch'), may hold values from 9.765625e-05 to 0.034
Outputs:
- output: bfloat16 [2048, 8192], P(('grp', 'ctx'), 'ch'), parts along dimension 0
- grad_qkv: bfloat16 [2048, 3, 8192], P(('grp', 'ctx'), None, 'ch'), parts along dimension 0
- grad_res: float32 [1024, 16], P(('grp', 'ch')), parts along dimension 0
The draws below stay inside these ranges and needn't reach their ends.
There are 2 independent parts, one for each index of `grp`. The reference program is written for one: setup_inputs(seed, part) draws one part's arguments, and reference() takes and returns one part's arrays. A program takes and returns all parts, laid end to end along the dimension named above; an argument that names none is the same for every part. Nothing has to cross between parts.
All inputs are finite; a program needn't handle non-finite values.
Results may differ from the reference program's by a relative error of at most 0.005.
Values sent between devices are 32-bit elements; how exact they have to be, the bound alone decides.
A program may use at most 128 MiB of HBM per device.

```python
import math
import jax
import jax.numpy as jnp
from jax import lax

D = 8192
GROUP = 16
ORDER = 16
SEQ = 1024
FG = 512


def mode_rates(key):
    pick_key, slow_key, wide_key, spare_key = jax.random.split(key, 4)
    slow_share = 0.5
    slow_pick = jax.random.uniform(pick_key, (FG, ORDER), jnp.float32) < slow_share
    slow_span = min(20.0, 0.034 * SEQ / 0.1)
    slow_rate = 0.1 / SEQ * jnp.exp(jax.random.uniform(slow_key, (FG, ORDER), jnp.float32) * math.log(slow_span))
    low_edge = min(2.0 / SEQ, 0.002)
    wide_rate = low_edge * jnp.exp(jax.random.uniform(wide_key, (FG, ORDER), jnp.float32) * math.log(0.034 / low_edge))
    return (jnp.where(slow_pick, slow_rate, wide_rate), spare_key)


def draw_residue(key, part):
    mode_rate, spare_key = mode_rates(jax.random.fold_in(key, 7))
    base_draw = jnp.clip(jax.random.normal(spare_key, (FG, ORDER), jnp.float32), -4.0, 4.0)
    return (base_draw * jnp.sqrt(2.0 * mode_rate) * 0.25).astype(jnp.float32)


def draw_decay(key, part):
    mode_rate, spare_key = mode_rates(jax.random.fold_in(key, 7))
    return mode_rate.astype(jnp.float32)


def block_levels(stream_key, shape, shards, least, top_value):
    gain, own = 1.0, jax.random.fold_in(stream_key, 6)
    for dim, parts in shards:
        draws = jnp.exp(jax.random.uniform(jax.random.fold_in(own, dim), (parts,), jnp.float32, least / len(shards), top_value / len(shards)))
        gain = gain * jnp.repeat(draws, shape[dim] // parts).reshape([-1 if axis == dim else 1 for axis in range(len(shape))])
    return gain


def noise(stream_key, shape, deviation, reach, cuts=(), dtype=jnp.bfloat16):
    loudness = block_levels(stream_key, shape, cuts, -0.22, 0.18) if cuts else 1.0
    values = jax.random.normal(stream_key, shape, jnp.float32) * deviation * loudness
    return jnp.minimum(jnp.maximum(values, -reach), reach).astype(dtype)


def setup_inputs(seed: int = 0, part: int = 0) -> dict:
    arg_keys = jax.random.split(jax.random.key(seed), 5)
    part_keys = jax.random.split(jax.random.fold_in(arg_keys[4], part), 5)
    qkv = noise(part_keys[0], (SEQ, 3, D), 1.0, 6.0, ((0, 8), (2, 2)))
    g_out = noise(part_keys[1], (SEQ, D), 1.0, 6.0, ((0, 8), (1, 2)))
    residue = draw_residue(jax.random.fold_in(arg_keys[4], 71), part)
    decay = draw_decay(jax.random.fold_in(arg_keys[4], 71), part)
    return {"qkv": qkv, "g_out": g_out, "residue": residue, "decay": decay}


def widen_groups(group_table):
    return jnp.repeat(group_table, GROUP, axis=-1)


def group_total(values):
    return values.reshape(values.shape[0], -1, GROUP).sum(axis=2)


def reference(qkv, g_out, residue, decay):
    channels = qkv.shape[2]
    query_part = qkv[:, 0].astype(jnp.float32)
    key_part = qkv[:, 1].astype(jnp.float32)
    value_part = qkv[:, 2].astype(jnp.float32)
    signal = lax.optimization_barrier((key_part * value_part).astype(jnp.bfloat16)).astype(jnp.float32)
    upstream = g_out.astype(jnp.float32)
    cotangent = lax.optimization_barrier((upstream * query_part).astype(jnp.bfloat16)).astype(jnp.float32)
    factor = widen_groups(jnp.exp(-decay).T)
    weight = widen_groups(residue.T)

    def modal_step(mode_state, signal_row):
        mode_state = factor * mode_state + signal_row[None, :]
        return mode_state, jnp.sum(weight * mode_state, axis=0)

    start_state = jnp.zeros((ORDER, channels), jnp.float32)
    _, mixed_sum = lax.scan(modal_step, start_state, signal)
    _, grad_signal = lax.scan(modal_step, start_state, cotangent, reverse=True)
    output = (query_part * mixed_sum).astype(jnp.bfloat16)

    def residue_step(running, rows_pair):
        mode_state, products = running
        signal_row, cotangent_row = rows_pair
        mode_state = factor * mode_state + signal_row[None, :]
        return (mode_state, products + mode_state * cotangent_row[None, :]), None

    (_, products), _ = lax.scan(residue_step, (start_state, start_state), (signal, cotangent))
    grad_res = group_total(products).T
    grad_qkv = jnp.stack([upstream * mixed_sum, grad_signal * value_part, grad_signal * key_part], 1).astype(jnp.bfloat16)
    return (output, grad_qkv, grad_res)
```

```python
import functools
import jax
import jax.numpy as jnp
from jax import lax
from jax.experimental import pallas as pl
from jax.experimental.pallas import tpu as pltpu
from jax.sharding import PartitionSpec as P

GROUP = 16
ORDER = 16
LANES = 256
PER = LANES // GROUP
ROWS = PER * ORDER
bf16 = jnp.bfloat16
f32 = jnp.float32
PAIR = 2


def split(a):
    hi = a.astype(bf16)
    return hi, (a - hi.astype(f32)).astype(bf16)


def mm(a, b, ca=1, cb=0):
    return lax.dot_general(a, b, (((ca,), (cb,)), ((), ())), preferred_element_type=f32)


def mm3(a, b, ca=1, cb=0):
    ah, al = split(a)
    bh, bl = split(b)
    return mm(ah, bh, ca, cb) + (mm(ah, bl, ca, cb) + mm(al, bh, ca, cb))


def iota(shape, dim):
    return lax.broadcasted_iota(jnp.int32, shape, dim)


def kernel(
    n, nb, per_chunk, length,
    q_ref, k_ref, v_ref, g_ref, d_ref, r_ref, drep_ref,
    out_ref, dq_ref, dk_ref, dv_ref, gr_ref,
    sig, cot, w0, w1, mix, gsig, own, peer, zf_in, zf_out, zb_in, zb_out, lags, gr_own, gr_all,
    xs, xr, fs, fr, bs, br, gs, grs,
):
    me = lax.axis_index("ctx")
    side = lax.rem(me, PAIR)
    z = me // PAIR
    nz = n // PAIR
    nc = nb // per_chunk
    partner = me + 1 - 2 * side
    half = 128

    barrier = pltpu.get_barrier_semaphore()

    def greet(i, c):
        pl.semaphore_signal(barrier, inc=1, device_id={"ctx": lax.rem(me + i, n)}, device_id_type=pl.DeviceIdType.MESH)
        return c

    lax.fori_loop(1, n, greet, 0)

    diag = (iota((ROWS, LANES), 0) // ORDER) == (iota((ROWS, LANES), 1) // GROUP)

    def states(j, c):
        cols = pl.ds(pl.multiple_of(j * LANES, LANES), LANES)
        sg = (k_ref[:, cols].astype(f32) * v_ref[:, cols].astype(f32)).astype(bf16)
        ct = (g_ref[:, cols].astype(f32) * q_ref[:, cols].astype(f32)).astype(bf16)
        sig[:, cols] = sg
        cot[:, cols] = ct
        d = d_ref[j]
        t = iota((length, LANES), 0).astype(f32)
        a0 = jnp.exp(-d * t)
        a1 = jnp.exp(-d * (length - t))
        w0[:, cols] = a0
        w1[:, cols] = a1
        for which, (a, x) in enumerate(((a1, sg), (a0, ct))):
            hi, lo = split(a.T)
            full = mm(hi, x) + mm(lo, x)
            own[j, which] = jnp.sum(jnp.where(diag, full, 0.0).reshape(PER, ORDER, LANES), axis=0)
        return c

    def xcopy(i):
        rows = pl.ds(i * per_chunk, per_chunk)
        return pltpu.make_async_remote_copy(
            src_ref=own.at[rows], dst_ref=peer.at[rows], send_sem=xs.at[i], recv_sem=xr.at[i],
            device_id={"ctx": partner}, device_id_type=pl.DeviceIdType.MESH)

    def zcopy(i, up):
        rows = pl.ds(i * per_chunk, per_chunk)
        src, dst, s, r = (zf_out, zf_in, fs, fr) if up else (zb_out, zb_in, bs, br)
        to = lax.rem(me + PAIR, n) if up else lax.rem(me + n - PAIR, n)
        return pltpu.make_async_remote_copy(
            src_ref=src.at[rows], dst_ref=dst.at[rows], send_sem=s.at[i], recv_sem=r.at[i],
            device_id={"ctx": to}, device_id_type=pl.DeviceIdType.MESH)

    def first(i, c):
        for u in range(per_chunk):
            states(i * per_chunk + u, 0)
        xcopy(i).start()
        return c

    pl.semaphore_wait(barrier, n - 1)
    lax.fori_loop(0, nc, first, 0)

    def fade(j):
        return jnp.exp(-drep_ref[:, pl.ds(pl.multiple_of(j * LANES, LANES), LANES)] * float(length))

    lower = iota((length, length), 1) <= iota((length, length), 0)
    upper = iota((length, length), 1) >= iota((length, length), 0)
    across = iota((length, length), 0) + iota((length, length), 1)
    corner = across <= length - 1
    flip = jnp.where(across == length - 1, 1.0, 0.0).astype(bf16)
    pick = (iota((PER, ROWS), 1) // ORDER) == iota((PER, ROWS), 0)
    pick16 = jnp.where(pick, 1.0, 0.0).astype(bf16)

    def heavy(j):
        cols = pl.ds(pl.multiple_of(j * LANES, LANES), LANES)
        r = r_ref[j]
        a0 = w0[:, cols]
        a1 = w1[:, cols]
        row0 = iota((length, LANES), 0) == 0
        h0, l0 = split(r * a0)
        h1, l1 = split(r * jnp.where(row0, 1.0, a1))
        h = mm(pick16, h0, 1, 1) + mm(pick16, l0, 1, 1)
        hr = mm(pick16, h1, 1, 1) + mm(pick16, l1, 1, 1)
        for p in range(LANES // half):
            hc = pl.ds(pl.multiple_of(j * LANES + p * half, half), half)
            sg = sig[:, hc]
            ct = cot[:, hc]
            back = mm(flip, ct)
            lane_group = iota((length, half), 1) // GROUP
            macc = jnp.zeros((length, half), f32)
            gacc = jnp.zeros((length, half), f32)
            for e in range(half // GROUP):
                g = p * (half // GROUP) + e
                tt = pltpu.roll(jnp.broadcast_to(h[g:g + 1], (length, length)), 0, 1, stride=1, stride_axis=0)
                tt = jnp.where(upper, tt, 0.0).astype(bf16)
                gacc = jnp.where(lane_group == e, mm(tt, ct), gacc)
                tf = pltpu.roll(jnp.broadcast_to(hr[g:g + 1], (length, length)), 0, 1, stride=1, stride_axis=0)
                tf = jnp.where(lower, tf, 0.0).astype(bf16)
                macc = jnp.where(lane_group == e, mm(tf, sg), macc)
                cm = jnp.where(lane_group == e, back, 0.0).astype(bf16)
                m = jnp.where(corner, mm(cm, sg, 1, 1), 0.0)
                m = pltpu.roll(m, 0, 1, stride=1, stride_axis=0)
                lags[g:g + 1, :] = jnp.sum(m, axis=0, keepdims=True)
            mix[:, hc] = macc
            gsig[:, hc] = gacc
        full = mm3(lags[...], jnp.exp(-d_ref[j] * (length - 1 - iota((length, LANES), 0)).astype(f32)))
        gr_own[pl.ds(j, 1)] = jnp.sum(jnp.where(pick, full, 0.0), axis=0, keepdims=True).reshape(1, 1, LANES)

    steps = max(nb, nc + nz)

    def comm(step):
        i = step - z

        @pl.when((i >= 0) & (i < nc))
        def _():
            @pl.when(z > 0)
            def _():
                zcopy(i, True).wait_recv()

            @pl.when(z < nz - 1)
            def _():
                for u in range(per_chunk):
                    j = i * per_chunk + u
                    f = fade(j)
                    mine, other = own[j, 0], peer[j, 0]
                    pair = jnp.where(side == 0, f * mine + other, f * other + mine)
                    zf_out[j] = pair + jnp.where(z > 0, f * f * zf_in[j], 0.0)
                zcopy(i, True).start()

        i2 = step - (nz - 1 - z)

        @pl.when((i2 >= 0) & (i2 < nc))
        def _():
            @pl.when(z < nz - 1)
            def _():
                zcopy(i2, False).wait_recv()

            @pl.when(z > 0)
            def _():
                for u in range(per_chunk):
                    j = i2 * per_chunk + u
                    f = fade(j)
                    mine, other = own[j, 1], peer[j, 1]
                    pair = jnp.where(side == 0, mine + f * other, other + f * mine)
                    zb_out[j] = pair + jnp.where(z < nz - 1, f * f * zb_in[j], 0.0)
                zcopy(i2, False).start()

    @pl.when(z == 0)
    def _():
        zf_in[...] = jnp.zeros_like(zf_in)

    @pl.when(z == nz - 1)
    def _():
        zb_in[...] = jnp.zeros_like(zb_in)

    def second(s, c):
        @pl.when(s < nb)
        def _():
            heavy(s)

        @pl.when((s >= 1) & (s - 1 < nc))
        def _():
            xcopy(s - 1).wait_recv()

        @pl.when(s >= 1)
        def _():
            comm(s - 1)

        return c

    lax.fori_loop(0, steps, second, 0)

    def carries(j, c):
        f = fade(j)
        zf, zb = zf_in[j], zb_in[j]
        cf = jnp.where(side == 0, zf, f * zf + peer[j, 0])
        cb = jnp.where(side == 0, f * zb + peer[j, 1], zb)
        zf_in[j] = cf
        zb_in[j] = cb
        hi, lo = split(own[j, 1] * cf)
        cross = mm(hi, pick16, 1, 1) + mm(lo, pick16, 1, 1)
        gr_own[nb + j] = fold(cross)
        return c

    def fold(cross):
        spread = mm3(cross, jnp.where(pick, 1.0, 0.0))
        keep = lax.rem(iota((ORDER, ROWS), 1), ORDER) == iota((ORDER, ROWS), 0)
        return jnp.sum(jnp.where(keep, spread, 0.0), axis=0, keepdims=True)

    lax.fori_loop(0, nb, carries, 0)

    def gcopy(i):
        to = lax.rem(me + i, n)
        return pltpu.make_async_remote_copy(
            src_ref=gr_own, dst_ref=gr_all.at[i], send_sem=gs.at[i], recv_sem=grs.at[i],
            device_id={"ctx": to}, device_id_type=pl.DeviceIdType.MESH)

    def gstart(i, c):
        gcopy(i).start()
        return c

    lax.fori_loop(1, n, gstart, 0)

    def last(j, c):
        cols = pl.ds(pl.multiple_of(j * LANES, LANES), LANES)
        r = r_ref[j]
        cf = jnp.where(diag, jnp.concatenate([zf_in[j]] * PER, 0), 0.0)
        cb = jnp.where(diag, jnp.concatenate([zb_in[j]] * PER, 0), 0.0)
        m = mix[:, cols] + mm3(r * w0[:, cols], cf)
        gsv = gsig[:, cols] + mm3(r * w1[:, cols], cb)
        out_ref[:, cols] = (q_ref[:, cols].astype(f32) * m).astype(bf16)
        dq_ref[:, cols] = (g_ref[:, cols].astype(f32) * m).astype(bf16)
        dk_ref[:, cols] = (gsv * v_ref[:, cols].astype(f32)).astype(bf16)
        dv_ref[:, cols] = (gsv * k_ref[:, cols].astype(f32)).astype(bf16)
        return c

    lax.fori_loop(0, nb, last, 0)

    def xend(i, c):
        xcopy(i).wait_send()

        @pl.when(z < nz - 1)
        def _():
            zcopy(i, True).wait_send()

        @pl.when(z > 0)
        def _():
            zcopy(i, False).wait_send()

        return c

    lax.fori_loop(0, nc, xend, 0)

    def gend(i, c):
        gcopy(i).wait()
        return c

    lax.fori_loop(1, n, gend, 0)

    def gsum(i, acc):
        return acc + gr_all[i]

    gr_ref[...] = lax.fori_loop(1, n, gsum, gr_own[...])


def on_device(n, qkv, g_out, residue, decay):
    length, _, channels = qkv.shape
    nb = channels // LANES
    per_chunk = 2
    nc = nb // per_chunk
    q, k, v = qkv[:, 0], qkv[:, 1], qkv[:, 2]
    d_row = decay.reshape(nb, 1, ROWS)
    r_row = residue.reshape(nb, 1, ROWS)
    drep = jnp.repeat(decay.T, GROUP, axis=1)
    wide = jax.ShapeDtypeStruct((length, channels), bf16)
    vm = pl.BlockSpec(memory_space=pltpu.VMEM)
    dma = pltpu.SemaphoreType.DMA
    out, dq, dk, dv, gr = pl.pallas_call(
        functools.partial(kernel, n, nb, per_chunk, length),
        out_shape=(wide, wide, wide, wide, jax.ShapeDtypeStruct((2 * nb, 1, ROWS), f32)),
        in_specs=[vm] * 7,
        out_specs=(vm,) * 5,
        scratch_shapes=[
            pltpu.VMEM((length, channels), bf16),
            pltpu.VMEM((length, channels), bf16),
            pltpu.VMEM((length, channels), f32),
            pltpu.VMEM((length, channels), f32),
            pltpu.VMEM((length, channels), f32),
            pltpu.VMEM((length, channels), f32),
            pltpu.VMEM((nb, 2, ORDER, LANES), f32),
            pltpu.VMEM((nb, 2, ORDER, LANES), f32),
            pltpu.VMEM((nb, ORDER, LANES), f32),
            pltpu.VMEM((nb, ORDER, LANES), f32),
            pltpu.VMEM((nb, ORDER, LANES), f32),
            pltpu.VMEM((nb, ORDER, LANES), f32),
            pltpu.VMEM((PER, length), f32),
            pltpu.VMEM((2 * nb, 1, ROWS), f32),
            pltpu.VMEM((n, 2 * nb, 1, ROWS), f32),
            dma((nc,)), dma((nc,)), dma((nc,)), dma((nc,)), dma((nc,)), dma((nc,)),
            dma((n,)), dma((n,)),
        ],
        compiler_params=pltpu.CompilerParams(
            collective_id=0, has_side_effects=True, vmem_limit_bytes=56 * 1024 * 1024),
    )(q, k, v, g_out, d_row, r_row, drep)
    grad_res = (gr[:nb] + gr[nb:]).reshape(nb * PER, ORDER)
    return out, jnp.stack([dq, dk, dv], 1), grad_res


def solution(mesh):
    return jax.shard_map(
        functools.partial(on_device, mesh.shape["ctx"]),
        mesh=mesh,
        in_specs=(
            P(("grp", "ctx"), None, "ch"),
            P(("grp", "ctx"), "ch"),
            P("ch", None),
            P("ch", None),
        ),
        out_specs=(P(("grp", "ctx"), "ch"), P(("grp", "ctx"), None, "ch"), P(("grp", "ch"), None)),
        check_vma=False,
    )
```

```python
import functools
import jax
import jax.numpy as jnp
from jax import lax
from jax.experimental import pallas as pl
from jax.experimental.pallas import tpu as pltpu
from jax.sharding import PartitionSpec as P

GROUP = 16
ORDER = 16
LANES = 256
PER = LANES // GROUP
ROWS = PER * ORDER
bf16 = jnp.bfloat16
f32 = jnp.float32
PAIR = 2


def split(a):
    hi = a.astype(bf16)
    return hi, (a - hi.astype(f32)).astype(bf16)


def mm(a, b, ca=1, cb=0):
    return lax.dot_general(a, b, (((ca,), (cb,)), ((), ())), preferred_element_type=f32)


def mm3(a, b, ca=1, cb=0):
    ah, al = split(a)
    bh, bl = split(b)
    return mm(ah, bh, ca, cb) + (mm(ah, bl, ca, cb) + mm(al, bh, ca, cb))


def iota(shape, dim):
    return lax.broadcasted_iota(jnp.int32, shape, dim)


def kernel(
    n, nb, per_chunk, length,
    x_ref, g_ref, dt_ref, rt_ref,
    out_ref, dx_ref, gr_ref,
    sig, cot, w0, w1, mix, gsig, own, peer, zf_in, zf_out, zb_in, zb_out, lags, gr_own, gr_all, drep, d_row, r_row, own_row, tmat,
    xs, xr, fs, fr, bs, br, gs, grs,
):
    me = lax.axis_index("ctx")
    side = lax.rem(me, PAIR)
    z = me // PAIR
    nz = n // PAIR
    nc = nb // per_chunk
    partner = me + 1 - 2 * side
    half = 128

    barrier = pltpu.get_barrier_semaphore()

    def greet(i, c):
        pl.semaphore_signal(barrier, inc=1, device_id={"ctx": lax.rem(me + i, n)}, device_id_type=pl.DeviceIdType.MESH)
        return c

    lax.fori_loop(1, n, greet, 0)

    diag = (iota((ROWS, LANES), 0) // ORDER) == (iota((ROWS, LANES), 1) // GROUP)

    def chosen(j):
        groups = nb * PER
        hit = iota((groups, LANES), 0) == j * PER + iota((groups, LANES), 1) // GROUP
        return jnp.where(hit, 1.0, 0.0).astype(bf16)

    def spread(table, j):
        hi = table.astype(bf16)
        rest = table - hi.astype(f32)
        mid = rest.astype(bf16)
        low = (rest - mid.astype(f32)).astype(bf16)
        hot = chosen(j)
        return mm(hi, hot) + mm(mid, hot) + mm(low, hot)

    def states(j, c):
        cols = pl.ds(pl.multiple_of(j * LANES, LANES), LANES)
        sg = (x_ref[1, :, cols].astype(f32) * x_ref[2, :, cols].astype(f32)).astype(bf16)
        ct = (g_ref[:, cols].astype(f32) * x_ref[0, :, cols].astype(f32)).astype(bf16)
        sig[:, cols] = sg
        cot[:, cols] = ct
        wide = spread(dt_ref[...], j)
        own_mode = lax.rem(iota((ORDER, LANES), 1), ORDER) == iota((ORDER, LANES), 0)
        drep[j] = jnp.exp(-wide * float(length))
        d = jnp.sum(jnp.where(own_mode, wide, 0.0), axis=0, keepdims=True)
        d_row[j] = d
        r_row[j] = jnp.sum(jnp.where(own_mode, spread(rt_ref[...], j), 0.0), axis=0, keepdims=True)
        t = iota((length, LANES), 0).astype(f32)
        a0 = jnp.exp(-d * t)
        a1 = jnp.exp(-d * (length - t))
        w0[:, cols] = a0
        w1[:, cols] = a1
        for which, (a, x) in enumerate(((a1, sg), (a0, ct))):
            hi, lo = split(a.T)
            full = mm(hi, x) + mm(lo, x)
            own[j, which] = jnp.sum(jnp.where(diag, full, 0.0).reshape(PER, ORDER, LANES), axis=0)
        return c

    def xcopy(i):
        rows = pl.ds(i * per_chunk, per_chunk)
        return pltpu.make_async_remote_copy(
            src_ref=own.at[rows], dst_ref=peer.at[rows], send_sem=xs.at[i], recv_sem=xr.at[i],
            device_id={"ctx": partner}, device_id_type=pl.DeviceIdType.MESH)

    def zcopy(i, up):
        rows = pl.ds(i * per_chunk, per_chunk)
        src, dst, s, r = (zf_out, zf_in, fs, fr) if up else (zb_out, zb_in, bs, br)
        to = lax.rem(me + PAIR, n) if up else lax.rem(me + n - PAIR, n)
        return pltpu.make_async_remote_copy(
            src_ref=src.at[rows], dst_ref=dst.at[rows], send_sem=s.at[i], recv_sem=r.at[i],
            device_id={"ctx": to}, device_id_type=pl.DeviceIdType.MESH)

    def first(i, c):
        for u in range(per_chunk):
            states(i * per_chunk + u, 0)
        xcopy(i).start()
        return c

    pl.semaphore_wait(barrier, n - 1)
    lax.fori_loop(0, nc, first, 0)

    def fade(j):
        return drep[j]

    lower = iota((length, length), 1) <= iota((length, length), 0)
    upper = iota((length, length), 1) >= iota((length, length), 0)
    across = iota((length, length), 0) + iota((length, length), 1)
    corner = across <= length - 1
    flip = jnp.where(across == length - 1, 1.0, 0.0).astype(bf16)
    pick = (iota((PER, ROWS), 1) // ORDER) == iota((PER, ROWS), 0)
    pick16 = jnp.where(pick, 1.0, 0.0).astype(bf16)

    def heavy(j):
        cols = pl.ds(pl.multiple_of(j * LANES, LANES), LANES)
        r = r_row[j]
        a0 = w0[:, cols]
        a1 = w1[:, cols]
        row0 = iota((length, LANES), 0) == 0
        h0, l0 = split(r * a0)
        h1, l1 = split(r * jnp.where(row0, 1.0, a1))
        h = mm(pick16, h0, 1, 1) + mm(pick16, l0, 1, 1)
        hr = mm(pick16, h1, 1, 1) + mm(pick16, l1, 1, 1)
        for p in range(LANES // half):
            hc = pl.ds(pl.multiple_of(j * LANES + p * half, half), half)
            sg = sig[:, hc]
            ct = cot[:, hc]
            back = mm(flip, ct)
            lane_group = iota((length, half), 1) // GROUP
            back16 = back.astype(bf16)
            for e in range(half // GROUP):
                g = p * (half // GROUP) + e
                rows = pl.ds(e * length, length)
                tt = pltpu.roll(jnp.broadcast_to(h[g:g + 1], (length, length)), 0, 1, stride=1, stride_axis=0)
                tmat[0, rows] = jnp.where(upper, tt, 0.0).astype(bf16)
                tf = pltpu.roll(jnp.broadcast_to(hr[g:g + 1], (length, length)), 0, 1, stride=1, stride_axis=0)
                tmat[1, rows] = jnp.where(lower, tf, 0.0).astype(bf16)
                tmat[2, rows] = back16 * jnp.where(iota((1, half), 1) // GROUP == e, 1.0, 0.0).astype(bf16)
            gall = mm(tmat[0], ct)
            mall = mm(tmat[1], sg)
            pall = mm(tmat[2], sg, 1, 1)
            gacc = gall[:length]
            macc = mall[:length]
            for e in range(half // GROUP):
                g = p * (half // GROUP) + e
                at = slice(e * length, (e + 1) * length)
                if e:
                    gacc = jnp.where(lane_group == e, gall[at], gacc)
                    macc = jnp.where(lane_group == e, mall[at], macc)
                m = pltpu.roll(jnp.where(corner, pall[at], 0.0), 0, 1, stride=1, stride_axis=0)
                lags[g:g + 1, :] = jnp.sum(m, axis=0, keepdims=True)
            mix[:, hc] = macc
            gsig[:, hc] = gacc
        full = mm3(lags[...], jnp.exp(-d_row[j] * (length - 1 - iota((length, LANES), 0)).astype(f32)))
        own_row[j] = jnp.sum(jnp.where(pick, full, 0.0), axis=0, keepdims=True)

    steps = max(nb, nc + nz)

    def comm(step):
        i = step - z

        @pl.when((i >= 0) & (i < nc))
        def _():
            @pl.when(z > 0)
            def _():
                zcopy(i, True).wait_recv()

            @pl.when(z < nz - 1)
            def _():
                for u in range(per_chunk):
                    j = i * per_chunk + u
                    f = fade(j)
                    mine, other = own[j, 0], peer[j, 0]
                    pair = jnp.where(side == 0, f * mine + other, f * other + mine)
                    zf_out[j] = pair + jnp.where(z > 0, f * f * zf_in[j], 0.0)
                zcopy(i, True).start()

        i2 = step - (nz - 1 - z)

        @pl.when((i2 >= 0) & (i2 < nc))
        def _():
            @pl.when(z < nz - 1)
            def _():
                zcopy(i2, False).wait_recv()

            @pl.when(z > 0)
            def _():
                for u in range(per_chunk):
                    j = i2 * per_chunk + u
                    f = fade(j)
                    mine, other = own[j, 1], peer[j, 1]
                    pair = jnp.where(side == 0, mine + f * other, other + f * mine)
                    zb_out[j] = pair + jnp.where(z < nz - 1, f * f * zb_in[j], 0.0)
                zcopy(i2, False).start()

    @pl.when(z == 0)
    def _():
        zf_in[...] = jnp.zeros_like(zf_in)

    @pl.when(z == nz - 1)
    def _():
        zb_in[...] = jnp.zeros_like(zb_in)

    def second(s, c):
        @pl.when(s < nb)
        def _():
            heavy(s)

        @pl.when((s >= 1) & (s - 1 < nc))
        def _():
            xcopy(s - 1).wait_recv()

        @pl.when(s >= 1)
        def _():
            comm(s - 1)

        return c

    lax.fori_loop(0, steps, second, 0)

    def carries(j, acc):
        f = fade(j)
        zf, zb = zf_in[j], zb_in[j]
        cf = jnp.where(side == 0, zf, f * zf + peer[j, 0])
        cb = jnp.where(side == 0, f * zb + peer[j, 1], zb)
        zf_in[j] = cf
        zb_in[j] = cb
        own_mode = lax.rem(iota((ORDER, LANES), 1), ORDER) == iota((ORDER, LANES), 0)
        hi, lo = split(own[j, 1] * cf + jnp.where(own_mode, own_row[j], 0.0))
        hot = chosen(j)
        return acc + mm(hi, hot, 1, 1) + mm(lo, hot, 1, 1)

    gr_own[...] = lax.fori_loop(0, nb, carries, jnp.zeros(gr_own.shape, f32))

    def gcopy(i):
        to = lax.rem(me + i, n)
        return pltpu.make_async_remote_copy(
            src_ref=gr_own, dst_ref=gr_all.at[i], send_sem=gs.at[i], recv_sem=grs.at[i],
            device_id={"ctx": to}, device_id_type=pl.DeviceIdType.MESH)

    def gstart(i, c):
        gcopy(i).start()
        return c

    lax.fori_loop(1, n, gstart, 0)

    def last(j, c):
        cols = pl.ds(pl.multiple_of(j * LANES, LANES), LANES)
        r = r_row[j]
        cf = jnp.where(diag, jnp.concatenate([zf_in[j]] * PER, 0), 0.0)
        cb = jnp.where(diag, jnp.concatenate([zb_in[j]] * PER, 0), 0.0)
        m = mix[:, cols] + mm3(r * w0[:, cols], cf)
        gsv = gsig[:, cols] + mm3(r * w1[:, cols], cb)
        out_ref[:, cols] = (x_ref[0, :, cols].astype(f32) * m).astype(bf16)
        dx_ref[0, :, cols] = (g_ref[:, cols].astype(f32) * m).astype(bf16)
        dx_ref[1, :, cols] = (gsv * x_ref[2, :, cols].astype(f32)).astype(bf16)
        dx_ref[2, :, cols] = (gsv * x_ref[1, :, cols].astype(f32)).astype(bf16)
        return c

    lax.fori_loop(0, nb, last, 0)

    def xend(i, c):
        xcopy(i).wait_send()

        @pl.when(z < nz - 1)
        def _():
            zcopy(i, True).wait_send()

        @pl.when(z > 0)
        def _():
            zcopy(i, False).wait_send()

        return c

    lax.fori_loop(0, nc, xend, 0)

    def gend(i, c):
        gcopy(i).wait()
        return c

    lax.fori_loop(1, n, gend, 0)

    def gsum(i, acc):
        return acc + gr_all[i]

    gr_ref[...] = lax.fori_loop(1, n, gsum, gr_own[...])


def on_device(n, qkv, g_out, residue, decay):
    length, _, channels = qkv.shape
    nb = channels // LANES
    per_chunk = 2
    nc = nb // per_chunk
    wide = jax.ShapeDtypeStruct((length, channels), bf16)
    vm = pl.BlockSpec(memory_space=pltpu.VMEM)
    dma = pltpu.SemaphoreType.DMA
    out, dx, gr = pl.pallas_call(
        functools.partial(kernel, n, nb, per_chunk, length),
        out_shape=(
            wide,
            jax.ShapeDtypeStruct((3, length, channels), bf16),
            jax.ShapeDtypeStruct((ORDER, nb * PER), f32),
        ),
        in_specs=[vm] * 4,
        out_specs=(vm,) * 3,
        scratch_shapes=[
            pltpu.VMEM((length, channels), bf16),
            pltpu.VMEM((length, channels), bf16),
            pltpu.VMEM((length, channels), f32),
            pltpu.VMEM((length, channels), f32),
            pltpu.VMEM((length, channels), f32),
            pltpu.VMEM((length, channels), f32),
            pltpu.VMEM((nb, 2, ORDER, LANES), f32),
            pltpu.VMEM((nb, 2, ORDER, LANES), f32),
            pltpu.VMEM((nb, ORDER, LANES), f32),
            pltpu.VMEM((nb, ORDER, LANES), f32),
            pltpu.VMEM((nb, ORDER, LANES), f32),
            pltpu.VMEM((nb, ORDER, LANES), f32),
            pltpu.VMEM((PER, length), f32),
            pltpu.VMEM((ORDER, nb * PER), f32),
            pltpu.VMEM((n, ORDER, nb * PER), f32),
            pltpu.VMEM((nb, ORDER, LANES), f32),
            pltpu.VMEM((nb, 1, LANES), f32),
            pltpu.VMEM((nb, 1, LANES), f32),
            pltpu.VMEM((nb, 1, LANES), f32),
            pltpu.VMEM((3, 8 * length, 128), bf16),
            dma((nc,)), dma((nc,)), dma((nc,)), dma((nc,)), dma((nc,)), dma((nc,)),
            dma((n,)), dma((n,)),
        ],
        compiler_params=pltpu.CompilerParams(
            collective_id=0, has_side_effects=True, vmem_limit_bytes=56 * 1024 * 1024),
    )(jnp.transpose(qkv, (1, 0, 2)), g_out, decay.T, residue.T)
    return out, jnp.transpose(dx, (1, 0, 2)), gr.T


def solution(mesh):
    return jax.shard_map(
        functools.partial(on_device, mesh.shape["ctx"]),
        mesh=mesh,
        in_specs=(
            P(("grp", "ctx"), None, "ch"),
            P(("grp", "ctx"), "ch"),
            P("ch", None),
            P("ch", None),
        ),
        out_specs=(P(("grp", "ctx"), "ch"), P(("grp", "ctx"), None, "ch"), P(("grp", "ch"), None)),
        check_vma=False,
    )
```

```python
import functools
import jax
import jax.numpy as jnp
from jax import lax
from jax.experimental import pallas as pl
from jax.experimental.pallas import tpu as pltpu
from jax.sharding import PartitionSpec as P

GROUP = 16
ORDER = 16
LANES = 256
PER = LANES // GROUP
ROWS = PER * ORDER
bf16 = jnp.bfloat16
f32 = jnp.float32
PAIR = 2
LEAD = 1
SLACK = 2


def split(a):
    hi = a.astype(bf16)
    return hi, (a - hi.astype(f32)).astype(bf16)


def mm(a, b, ca=1, cb=0):
    return lax.dot_general(a, b, (((ca,), (cb,)), ((), ())), preferred_element_type=f32)


def mm3(a, b, ca=1, cb=0):
    ah, al = split(a)
    bh, bl = split(b)
    return mm(ah, bh, ca, cb) + (mm(ah, bl, ca, cb) + mm(al, bh, ca, cb))


def iota(shape, dim):
    return lax.broadcasted_iota(jnp.int32, shape, dim)


def kernel(
    n, nb, per_chunk, length,
    x_ref, g_ref, dt_ref, rt_ref,
    out_ref, dx_ref, gr_ref,
    sig, cot, w0, w1, mix, gsig, own, peer, zf_in, zf_out, zb_in, zb_out, lags, gr_own, gr_all, drep, d_row, r_row, own_row, tmat,
    xs, xr, fs, fr, bs, br, gs, grs,
):
    me = lax.axis_index("ctx")
    side = lax.rem(me, PAIR)
    z = me // PAIR
    nz = n // PAIR
    nc = nb // per_chunk
    partner = me + 1 - 2 * side
    half = 128

    barrier = pltpu.get_barrier_semaphore()

    def greet(i, c):
        pl.semaphore_signal(barrier, inc=1, device_id={"ctx": lax.rem(me + i, n)}, device_id_type=pl.DeviceIdType.MESH)
        return c

    lax.fori_loop(1, n, greet, 0)

    diag = (iota((ROWS, LANES), 0) // ORDER) == (iota((ROWS, LANES), 1) // GROUP)

    def chosen(j):
        groups = nb * PER
        hit = iota((groups, LANES), 0) == j * PER + iota((groups, LANES), 1) // GROUP
        return jnp.where(hit, 1.0, 0.0).astype(bf16)

    def spread(table, j):
        hi = table.astype(bf16)
        rest = table - hi.astype(f32)
        mid = rest.astype(bf16)
        low = (rest - mid.astype(f32)).astype(bf16)
        hot = chosen(j)
        return mm(hi, hot) + mm(mid, hot) + mm(low, hot)

    def states(j, c):
        cols = pl.ds(pl.multiple_of(j * LANES, LANES), LANES)
        sg = (x_ref[1, :, cols].astype(f32) * x_ref[2, :, cols].astype(f32)).astype(bf16)
        ct = (g_ref[:, cols].astype(f32) * x_ref[0, :, cols].astype(f32)).astype(bf16)
        sig[:, cols] = sg
        cot[:, cols] = ct
        wide = spread(dt_ref[...], j)
        own_mode = lax.rem(iota((ORDER, LANES), 1), ORDER) == iota((ORDER, LANES), 0)
        drep[j] = jnp.exp(-wide * float(length))
        d = jnp.sum(jnp.where(own_mode, wide, 0.0), axis=0, keepdims=True)
        d_row[j] = d
        r_row[j] = jnp.sum(jnp.where(own_mode, spread(rt_ref[...], j), 0.0), axis=0, keepdims=True)
        t = iota((length, LANES), 0).astype(f32)
        a0 = jnp.exp(-d * t)
        a1 = jnp.exp(-d * (length - t))
        w0[:, cols] = a0
        w1[:, cols] = a1
        for which, (a, x) in enumerate(((a1, sg), (a0, ct))):
            hi, lo = split(a.T)
            full = mm(hi, x) + mm(lo, x)
            own[j, which] = jnp.sum(jnp.where(diag, full, 0.0).reshape(PER, ORDER, LANES), axis=0)
        return c

    def xcopy(i):
        rows = pl.ds(i * per_chunk, per_chunk)
        return pltpu.make_async_remote_copy(
            src_ref=own.at[rows], dst_ref=peer.at[rows], send_sem=xs.at[i], recv_sem=xr.at[i],
            device_id={"ctx": partner}, device_id_type=pl.DeviceIdType.MESH)

    def zcopy(i, up):
        rows = pl.ds(i * per_chunk, per_chunk)
        src, dst, s, r = (zf_out, zf_in, fs, fr) if up else (zb_out, zb_in, bs, br)
        to = lax.rem(me + PAIR, n) if up else lax.rem(me + n - PAIR, n)
        return pltpu.make_async_remote_copy(
            src_ref=src.at[rows], dst_ref=dst.at[rows], send_sem=s.at[i], recv_sem=r.at[i],
            device_id={"ctx": to}, device_id_type=pl.DeviceIdType.MESH)

    def first(i, c):
        for u in range(per_chunk):
            states(i * per_chunk + u, 0)
        xcopy(i).start()
        return c

    early = (3 * nc) // 4

    def ahead(j, c):
        states(j, 0)
        return c

    def send(i, c):
        xcopy(i).start()
        return c

    lax.fori_loop(0, early * per_chunk, ahead, 0)
    pl.semaphore_wait(barrier, n - 1)
    lax.fori_loop(0, early, send, 0)
    lax.fori_loop(early, nc, first, 0)

    def fade(j):
        return drep[j]

    lower = iota((length, length), 1) <= iota((length, length), 0)
    upper = iota((length, length), 1) >= iota((length, length), 0)
    across = iota((length, length), 0) + iota((length, length), 1)
    corner = across <= length - 1
    flip = jnp.where(across == length - 1, 1.0, 0.0).astype(bf16)
    pick = (iota((PER, ROWS), 1) // ORDER) == iota((PER, ROWS), 0)
    pick16 = jnp.where(pick, 1.0, 0.0).astype(bf16)

    def heavy(j):
        cols = pl.ds(pl.multiple_of(j * LANES, LANES), LANES)
        r = r_row[j]
        a0 = w0[:, cols]
        a1 = w1[:, cols]
        row0 = iota((length, LANES), 0) == 0
        h0, l0 = split(r * a0)
        h1, l1 = split(r * jnp.where(row0, 1.0, a1))
        h = mm(pick16, h0, 1, 1) + mm(pick16, l0, 1, 1)
        hr = mm(pick16, h1, 1, 1) + mm(pick16, l1, 1, 1)
        for p in range(LANES // half):
            hc = pl.ds(pl.multiple_of(j * LANES + p * half, half), half)
            sg = sig[:, hc]
            ct = cot[:, hc]
            back = mm(flip, ct)
            lane_group = iota((length, half), 1) // GROUP
            back16 = back.astype(bf16)
            for e in range(half // GROUP):
                g = p * (half // GROUP) + e
                rows = pl.ds(e * length, length)
                tt = pltpu.roll(jnp.broadcast_to(h[g:g + 1], (length, length)), 0, 1, stride=1, stride_axis=0)
                tmat[0, rows] = jnp.where(upper, tt, 0.0).astype(bf16)
                tf = pltpu.roll(jnp.broadcast_to(hr[g:g + 1], (length, length)), 0, 1, stride=1, stride_axis=0)
                tmat[1, rows] = jnp.where(lower, tf, 0.0).astype(bf16)
                tmat[2, rows] = back16 * jnp.where(iota((1, half), 1) // GROUP == e, 1.0, 0.0).astype(bf16)
            gall = mm(tmat[0], ct)
            mall = mm(tmat[1], sg)
            pall = mm(tmat[2], sg, 1, 1)
            gacc = gall[:length]
            macc = mall[:length]
            for e in range(half // GROUP):
                g = p * (half // GROUP) + e
                at = slice(e * length, (e + 1) * length)
                if e:
                    gacc = jnp.where(lane_group == e, gall[at], gacc)
                    macc = jnp.where(lane_group == e, mall[at], macc)
                m = pltpu.roll(jnp.where(corner, pall[at], 0.0), 0, 1, stride=1, stride_axis=0)
                lags[g:g + 1, :] = jnp.sum(m, axis=0, keepdims=True)
            mix[:, hc] = macc
            gsig[:, hc] = gacc
        full = mm3(lags[...], jnp.exp(-d_row[j] * (length - 1 - iota((length, LANES), 0)).astype(f32)))
        own_row[j] = jnp.sum(jnp.where(pick, full, 0.0), axis=0, keepdims=True)

    steps = max(nb, LEAD + nc + SLACK * (nz - 1))

    def comm(step):
        i = step - SLACK * z

        @pl.when((i >= 0) & (i < nc))
        def _():
            @pl.when(z > 0)
            def _():
                zcopy(i, True).wait_recv()

            @pl.when(z < nz - 1)
            def _():
                for u in range(per_chunk):
                    j = i * per_chunk + u
                    f = fade(j)
                    mine, other = own[j, 0], peer[j, 0]
                    pair = jnp.where(side == 0, f * mine + other, f * other + mine)
                    zf_out[j] = pair + jnp.where(z > 0, f * f * zf_in[j], 0.0)
                zcopy(i, True).start()

        i2 = step - SLACK * (nz - 1 - z)

        @pl.when((i2 >= 0) & (i2 < nc))
        def _():
            @pl.when(z < nz - 1)
            def _():
                zcopy(i2, False).wait_recv()

            @pl.when(z > 0)
            def _():
                for u in range(per_chunk):
                    j = i2 * per_chunk + u
                    f = fade(j)
                    mine, other = own[j, 1], peer[j, 1]
                    pair = jnp.where(side == 0, mine + f * other, other + f * mine)
                    zb_out[j] = pair + jnp.where(z < nz - 1, f * f * zb_in[j], 0.0)
                zcopy(i2, False).start()

    @pl.when(z == 0)
    def _():
        zf_in[...] = jnp.zeros_like(zf_in)

    @pl.when(z == nz - 1)
    def _():
        zb_in[...] = jnp.zeros_like(zb_in)

    def second(s, c):
        @pl.when(s < nb)
        def _():
            heavy(s)

        @pl.when((s >= LEAD) & (s - LEAD < nc))
        def _():
            xcopy(s - LEAD).wait_recv()

        @pl.when(s >= LEAD)
        def _():
            comm(s - LEAD)

        return c

    lax.fori_loop(0, steps, second, 0)

    def carries(j, acc):
        f = fade(j)
        zf, zb = zf_in[j], zb_in[j]
        cf = jnp.where(side == 0, zf, f * zf + peer[j, 0])
        cb = jnp.where(side == 0, f * zb + peer[j, 1], zb)
        zf_in[j] = cf
        zb_in[j] = cb
        own_mode = lax.rem(iota((ORDER, LANES), 1), ORDER) == iota((ORDER, LANES), 0)
        hi, lo = split(own[j, 1] * cf + jnp.where(own_mode, own_row[j], 0.0))
        hot = chosen(j)
        return acc + mm(hi, hot, 1, 1) + mm(lo, hot, 1, 1)

    gr_own[...] = lax.fori_loop(0, nb, carries, jnp.zeros(gr_own.shape, f32))

    def gcopy(i):
        to = lax.rem(me + i, n)
        return pltpu.make_async_remote_copy(
            src_ref=gr_own, dst_ref=gr_all.at[i], send_sem=gs.at[i], recv_sem=grs.at[i],
            device_id={"ctx": to}, device_id_type=pl.DeviceIdType.MESH)

    def gstart(i, c):
        gcopy(i).start()
        return c

    lax.fori_loop(1, n, gstart, 0)

    def last(j, c):
        cols = pl.ds(pl.multiple_of(j * LANES, LANES), LANES)
        r = r_row[j]
        cf = jnp.where(diag, jnp.concatenate([zf_in[j]] * PER, 0), 0.0)
        cb = jnp.where(diag, jnp.concatenate([zb_in[j]] * PER, 0), 0.0)
        m = mix[:, cols] + mm3(r * w0[:, cols], cf)
        gsv = gsig[:, cols] + mm3(r * w1[:, cols], cb)
        out_ref[:, cols] = (x_ref[0, :, cols].astype(f32) * m).astype(bf16)
        dx_ref[0, :, cols] = (g_ref[:, cols].astype(f32) * m).astype(bf16)
        dx_ref[1, :, cols] = (gsv * x_ref[2, :, cols].astype(f32)).astype(bf16)
        dx_ref[2, :, cols] = (gsv * x_ref[1, :, cols].astype(f32)).astype(bf16)
        return c

    lax.fori_loop(0, nb, last, 0)

    def xend(i, c):
        xcopy(i).wait_send()

        @pl.when(z < nz - 1)
        def _():
            zcopy(i, True).wait_send()

        @pl.when(z > 0)
        def _():
            zcopy(i, False).wait_send()

        return c

    lax.fori_loop(0, nc, xend, 0)

    def gend(i, c):
        gcopy(i).wait()
        return c

    lax.fori_loop(1, n, gend, 0)

    def gsum(i, acc):
        return acc + gr_all[i]

    gr_ref[...] = lax.fori_loop(1, n, gsum, gr_own[...])


def pass_on(a_ref, b_ref, c_ref, x_ref, y_ref, z_ref):
    x_ref[...] = a_ref[...]
    y_ref[...] = b_ref[...]
    z_ref[...] = c_ref[...]


def settle(out, dx, gr):
    length, channels = out.shape
    width = min(1024, channels)
    specs = (
        pl.BlockSpec((length, width), lambda i: (0, i)),
        pl.BlockSpec((3, length, width), lambda i: (0, 0, i)),
        pl.BlockSpec(gr.shape, lambda i: (0, 0)),
    )
    return pl.pallas_call(
        pass_on,
        grid=(channels // width,),
        out_shape=tuple(jax.ShapeDtypeStruct(a.shape, a.dtype) for a in (out, dx, gr)),
        in_specs=list(specs),
        out_specs=specs,
        compiler_params=pltpu.CompilerParams(vmem_limit_bytes=16 * 1024 * 1024),
    )(out, dx, gr)


def on_device(n, qkv, g_out, residue, decay):
    length, _, channels = qkv.shape
    nb = channels // LANES
    per_chunk = 2
    nc = nb // per_chunk
    wide = jax.ShapeDtypeStruct((length, channels), bf16)
    vm = pl.BlockSpec(memory_space=pltpu.VMEM)
    dma = pltpu.SemaphoreType.DMA
    out, dx, gr = pl.pallas_call(
        functools.partial(kernel, n, nb, per_chunk, length),
        out_shape=(
            wide,
            jax.ShapeDtypeStruct((3, length, channels), bf16),
            jax.ShapeDtypeStruct((ORDER, nb * PER), f32),
        ),
        in_specs=[vm] * 4,
        out_specs=(vm,) * 3,
        scratch_shapes=[
            pltpu.VMEM((length, channels), bf16),
            pltpu.VMEM((length, channels), bf16),
            pltpu.VMEM((length, channels), f32),
            pltpu.VMEM((length, channels), f32),
            pltpu.VMEM((length, channels), f32),
            pltpu.VMEM((length, channels), f32),
            pltpu.VMEM((nb, 2, ORDER, LANES), f32),
            pltpu.VMEM((nb, 2, ORDER, LANES), f32),
            pltpu.VMEM((nb, ORDER, LANES), f32),
            pltpu.VMEM((nb, ORDER, LANES), f32),
            pltpu.VMEM((nb, ORDER, LANES), f32),
            pltpu.VMEM((nb, ORDER, LANES), f32),
            pltpu.VMEM((PER, length), f32),
            pltpu.VMEM((ORDER, nb * PER), f32),
            pltpu.VMEM((n, ORDER, nb * PER), f32),
            pltpu.VMEM((nb, ORDER, LANES), f32),
            pltpu.VMEM((nb, 1, LANES), f32),
            pltpu.VMEM((nb, 1, LANES), f32),
            pltpu.VMEM((nb, 1, LANES), f32),
            pltpu.VMEM((3, 8 * length, 128), bf16),
            dma((nc,)), dma((nc,)), dma((nc,)), dma((nc,)), dma((nc,)), dma((nc,)),
            dma((n,)), dma((n,)),
        ],
        compiler_params=pltpu.CompilerParams(
            collective_id=0, has_side_effects=True, vmem_limit_bytes=40 * 1024 * 1024),
    )(jnp.transpose(qkv, (1, 0, 2)), g_out, decay.T, residue.T)
    out, dx, gr = settle(out, dx, gr)
    return out, jnp.transpose(dx, (1, 0, 2)), gr.T


def solution(mesh):
    return jax.shard_map(
        functools.partial(on_device, mesh.shape["ctx"]),
        mesh=mesh,
        in_specs=(
            P(("grp", "ctx"), None, "ch"),
            P(("grp", "ctx"), "ch"),
            P("ch", None),
            P("ch", None),
        ),
        out_specs=(P(("grp", "ctx"), "ch"), P(("grp", "ctx"), None, "ch"), P(("grp", "ch"), None)),
        check_vma=False,
    )
```

```python
import functools
import jax
import jax.numpy as jnp
from jax import lax
from jax.experimental import pallas as pl
from jax.experimental.pallas import tpu as pltpu
from jax.sharding import PartitionSpec as P

GROUP = 16
ORDER = 16
LANES = 256
PER = LANES // GROUP
ROWS = PER * ORDER
bf16 = jnp.bfloat16
f32 = jnp.float32
PAIR = 2
LEAD = 1
SLACK = 3


def split(a):
    hi = a.astype(bf16)
    return hi, (a - hi.astype(f32)).astype(bf16)


def mm(a, b, ca=1, cb=0):
    return lax.dot_general(a, b, (((ca,), (cb,)), ((), ())), preferred_element_type=f32)


def mm3(a, b, ca=1, cb=0):
    ah, al = split(a)
    bh, bl = split(b)
    return mm(ah, bh, ca, cb) + (mm(ah, bl, ca, cb) + mm(al, bh, ca, cb))


def iota(shape, dim):
    return lax.broadcasted_iota(jnp.int32, shape, dim)


def kernel(
    n, nb, per_chunk, length,
    x_hbm, g_hbm, dt_ref, rt_ref,
    out_ref, dx_ref, gr_ref,
    sig, cot, w0, w1, mix, gsig, own, peer, zf_in, zf_out, zb_in, zb_out, lags, gr_own, gr_all, drep, d_row, r_row, own_row, tmat, pmat, x_ref, g_ref,
    xs, xr, fs, fr, bs, br, gs, grs, xin, gin,
):
    me = lax.axis_index("ctx")
    side = lax.rem(me, PAIR)
    z = me // PAIR
    nz = n // PAIR
    nc = nb // per_chunk
    partner = me + 1 - 2 * side
    half = 128

    def load(i):
        cols = pl.ds(pl.multiple_of(i * per_chunk * LANES, LANES), per_chunk * LANES)
        return (
            pltpu.make_async_copy(x_hbm.at[:, :, cols], x_ref.at[:, :, cols], xin.at[i]),
            pltpu.make_async_copy(g_hbm.at[:, cols], g_ref.at[:, cols], gin.at[i]),
        )

    def load_start(i, c):
        for copy in load(i):
            copy.start()
        return c

    lax.fori_loop(0, nc, load_start, 0)
    barrier = pltpu.get_barrier_semaphore()

    def greet(i, c):
        pl.semaphore_signal(barrier, inc=1, device_id={"ctx": lax.rem(me + i, n)}, device_id_type=pl.DeviceIdType.MESH)
        return c

    lax.fori_loop(1, n, greet, 0)

    diag = (iota((ROWS, LANES), 0) // ORDER) == (iota((ROWS, LANES), 1) // GROUP)

    def chosen(j):
        groups = nb * PER
        hit = iota((groups, LANES), 0) == j * PER + iota((groups, LANES), 1) // GROUP
        return jnp.where(hit, 1.0, 0.0).astype(bf16)

    def spread(table, j):
        hi = table.astype(bf16)
        rest = table - hi.astype(f32)
        mid = rest.astype(bf16)
        low = (rest - mid.astype(f32)).astype(bf16)
        hot = chosen(j)
        return mm(hi, hot) + mm(mid, hot) + mm(low, hot)

    def states(j, c):
        cols = pl.ds(pl.multiple_of(j * LANES, LANES), LANES)
        sg = (x_ref[1, :, cols].astype(f32) * x_ref[2, :, cols].astype(f32)).astype(bf16)
        ct = (g_ref[:, cols].astype(f32) * x_ref[0, :, cols].astype(f32)).astype(bf16)
        sig[:, cols] = sg
        cot[:, cols] = ct
        wide = spread(dt_ref[...], j)
        own_mode = lax.rem(iota((ORDER, LANES), 1), ORDER) == iota((ORDER, LANES), 0)
        drep[j] = jnp.exp(-wide * float(length))
        d = jnp.sum(jnp.where(own_mode, wide, 0.0), axis=0, keepdims=True)
        d_row[j] = d
        r_row[j] = jnp.sum(jnp.where(own_mode, spread(rt_ref[...], j), 0.0), axis=0, keepdims=True)
        t = iota((length, LANES), 0).astype(f32)
        a0 = jnp.exp(-d * t)
        a1 = jnp.exp(-d * (length - t))
        w0[:, cols] = a0
        w1[:, cols] = a1
        for which, (a, x) in enumerate(((a1, sg), (a0, ct))):
            hi, lo = split(a.T)
            full = mm(hi, x) + mm(lo, x)
            own[j, which] = jnp.sum(jnp.where(diag, full, 0.0).reshape(PER, ORDER, LANES), axis=0)
        return c

    def xcopy(i):
        rows = pl.ds(i * per_chunk, per_chunk)
        return pltpu.make_async_remote_copy(
            src_ref=own.at[rows], dst_ref=peer.at[rows], send_sem=xs.at[i], recv_sem=xr.at[i],
            device_id={"ctx": partner}, device_id_type=pl.DeviceIdType.MESH)

    def zcopy(i, up):
        rows = pl.ds(i * per_chunk, per_chunk)
        src, dst, s, r = (zf_out, zf_in, fs, fr) if up else (zb_out, zb_in, bs, br)
        to = lax.rem(me + PAIR, n) if up else lax.rem(me + n - PAIR, n)
        return pltpu.make_async_remote_copy(
            src_ref=src.at[rows], dst_ref=dst.at[rows], send_sem=s.at[i], recv_sem=r.at[i],
            device_id={"ctx": to}, device_id_type=pl.DeviceIdType.MESH)

    def first(i, c):
        ahead(i, 0)
        xcopy(i).start()
        return c

    def ahead(i, c):
        for copy in load(i):
            copy.wait()
        for u in range(per_chunk):
            states(i * per_chunk + u, 0)
        return c

    early = (3 * nc) // 4

    def send(i, c):
        xcopy(i).start()
        return c

    lax.fori_loop(0, early, ahead, 0)
    pl.semaphore_wait(barrier, n - 1)
    lax.fori_loop(0, early, send, 0)
    lax.fori_loop(early, nc, first, 0)

    def fade(j):
        return drep[j]

    lower = iota((length, length), 1) <= iota((length, length), 0)
    upper = iota((length, length), 1) >= iota((length, length), 0)
    across = iota((length, length), 0) + iota((length, length), 1)
    corner = across <= length - 1
    flip = jnp.where(across == length - 1, 1.0, 0.0).astype(bf16)
    pick = (iota((PER, ROWS), 1) // ORDER) == iota((PER, ROWS), 0)
    pick16 = jnp.where(pick, 1.0, 0.0).astype(bf16)

    def heavy(j):
        cols = pl.ds(pl.multiple_of(j * LANES, LANES), LANES)
        r = r_row[j]
        a0 = w0[:, cols]
        a1 = w1[:, cols]
        row0 = iota((length, LANES), 0) == 0
        h0, l0 = split(r * a0)
        h1, l1 = split(r * jnp.where(row0, 1.0, a1))
        h = mm(pick16, h0, 1, 1) + mm(pick16, l0, 1, 1)
        hr = mm(pick16, h1, 1, 1) + mm(pick16, l1, 1, 1)
        blank = jnp.zeros((length, half), bf16)

        def corners(a, b):
            return jnp.concatenate(
                [jnp.concatenate([a, blank], 1), jnp.concatenate([blank, b], 1)], 0)

        sgw = sig[:, cols]
        ctw = cot[:, cols]
        back = mm(flip, ctw).astype(bf16)
        per_half = half // GROUP
        lane_group = iota((length, half), 1) // GROUP
        for e in range(per_half):
            keep = lax.rem(iota((1, LANES), 1) // GROUP, per_half) == e
            pmat[pl.ds(e * length, length)] = back * jnp.where(keep, 1.0, 0.0).astype(bf16)
        pall = mm(pmat[...], corners(sgw[:, :half], sgw[:, half:]), 1, 1)
        for p in range(LANES // half):
            hc = pl.ds(pl.multiple_of(j * LANES + p * half, half), half)
            side_cols = slice(p * half, (p + 1) * half)
            for e in range(per_half):
                g = p * per_half + e
                rows = pl.ds(e * length, length)
                tt = pltpu.roll(jnp.broadcast_to(h[g:g + 1], (length, length)), 0, 1, stride=1, stride_axis=0)
                tmat[p, rows, half:] = jnp.where(upper, tt, 0.0).astype(bf16)
                tf = pltpu.roll(jnp.broadcast_to(hr[g:g + 1], (length, length)), 0, 1, stride=1, stride_axis=0)
                tmat[p, rows, :half] = jnp.where(lower, tf, 0.0).astype(bf16)
            both = mm(tmat[p], corners(sgw[:, side_cols], ctw[:, side_cols]))
            macc = both[:length, :half]
            gacc = both[:length, half:]
            for e in range(per_half):
                g = p * per_half + e
                at = slice(e * length, (e + 1) * length)
                if e:
                    macc = jnp.where(lane_group == e, both[at, :half], macc)
                    gacc = jnp.where(lane_group == e, both[at, half:], gacc)
                m = pltpu.roll(jnp.where(corner, pall[at, side_cols], 0.0), 0, 1, stride=1, stride_axis=0)
                lags[g:g + 1, :] = jnp.sum(m, axis=0, keepdims=True)
            mix[:, hc] = macc
            gsig[:, hc] = gacc
        full = mm3(lags[...], jnp.exp(-d_row[j] * (length - 1 - iota((length, LANES), 0)).astype(f32)))
        own_row[j] = jnp.sum(jnp.where(pick, full, 0.0), axis=0, keepdims=True)

    steps = max(nb, LEAD + nc + SLACK * (nz - 1))

    def comm(step):
        i = step - SLACK * z

        @pl.when((i >= 0) & (i < nc))
        def _():
            @pl.when(z > 0)
            def _():
                zcopy(i, True).wait_recv()

            @pl.when(z < nz - 1)
            def _():
                for u in range(per_chunk):
                    j = i * per_chunk + u
                    f = fade(j)
                    mine, other = own[j, 0], peer[j, 0]
                    pair = jnp.where(side == 0, f * mine + other, f * other + mine)
                    zf_out[j] = pair + jnp.where(z > 0, f * f * zf_in[j], 0.0)
                zcopy(i, True).start()

        i2 = step - SLACK * (nz - 1 - z)

        @pl.when((i2 >= 0) & (i2 < nc))
        def _():
            @pl.when(z < nz - 1)
            def _():
                zcopy(i2, False).wait_recv()

            @pl.when(z > 0)
            def _():
                for u in range(per_chunk):
                    j = i2 * per_chunk + u
                    f = fade(j)
                    mine, other = own[j, 1], peer[j, 1]
                    pair = jnp.where(side == 0, mine + f * other, other + f * mine)
                    zb_out[j] = pair + jnp.where(z < nz - 1, f * f * zb_in[j], 0.0)
                zcopy(i2, False).start()

    @pl.when(z == 0)
    def _():
        zf_in[...] = jnp.zeros_like(zf_in)

    @pl.when(z == nz - 1)
    def _():
        zb_in[...] = jnp.zeros_like(zb_in)

    def second(s, c):
        @pl.when(s < nb)
        def _():
            heavy(s)

        @pl.when((s >= LEAD) & (s - LEAD < nc))
        def _():
            xcopy(s - LEAD).wait_recv()

        @pl.when(s >= LEAD)
        def _():
            comm(s - LEAD)

        return c

    lax.fori_loop(0, steps, second, 0)

    def carries(j, acc):
        f = fade(j)
        zf, zb = zf_in[j], zb_in[j]
        cf = jnp.where(side == 0, zf, f * zf + peer[j, 0])
        cb = jnp.where(side == 0, f * zb + peer[j, 1], zb)
        zf_in[j] = cf
        zb_in[j] = cb
        own_mode = lax.rem(iota((ORDER, LANES), 1), ORDER) == iota((ORDER, LANES), 0)
        hi, lo = split(own[j, 1] * cf + jnp.where(own_mode, own_row[j], 0.0))
        hot = chosen(j)
        return acc + mm(hi, hot, 1, 1) + mm(lo, hot, 1, 1)

    gr_own[...] = lax.fori_loop(0, nb, carries, jnp.zeros(gr_own.shape, f32), unroll=4)

    def gcopy(i):
        to = lax.rem(me + i, n)
        return pltpu.make_async_remote_copy(
            src_ref=gr_own, dst_ref=gr_all.at[i], send_sem=gs.at[i], recv_sem=grs.at[i],
            device_id={"ctx": to}, device_id_type=pl.DeviceIdType.MESH)

    def gstart(i, c):
        gcopy(i).start()
        return c

    lax.fori_loop(1, n, gstart, 0)

    def last(j, c):
        cols = pl.ds(pl.multiple_of(j * LANES, LANES), LANES)
        r = r_row[j]
        cf = jnp.where(diag, jnp.concatenate([zf_in[j]] * PER, 0), 0.0)
        cb = jnp.where(diag, jnp.concatenate([zb_in[j]] * PER, 0), 0.0)
        m = mix[:, cols] + mm3(r * w0[:, cols], cf)
        gsv = gsig[:, cols] + mm3(r * w1[:, cols], cb)
        out_ref[:, cols] = (x_ref[0, :, cols].astype(f32) * m).astype(bf16)
        dx_ref[0, :, cols] = (g_ref[:, cols].astype(f32) * m).astype(bf16)
        dx_ref[1, :, cols] = (gsv * x_ref[2, :, cols].astype(f32)).astype(bf16)
        dx_ref[2, :, cols] = (gsv * x_ref[1, :, cols].astype(f32)).astype(bf16)
        return c

    lax.fori_loop(0, nb, last, 0, unroll=2)

    def xend(i, c):
        xcopy(i).wait_send()

        @pl.when(z < nz - 1)
        def _():
            zcopy(i, True).wait_send()

        @pl.when(z > 0)
        def _():
            zcopy(i, False).wait_send()

        return c

    lax.fori_loop(0, nc, xend, 0)

    def gend(i, c):
        gcopy(i).wait()
        return c

    lax.fori_loop(1, n, gend, 0)

    def gsum(i, acc):
        return acc + gr_all[i]

    gr_ref[...] = lax.fori_loop(1, n, gsum, gr_own[...])


def pass_on(a_ref, b_ref, c_ref, x_ref, y_ref, z_ref):
    x_ref[...] = a_ref[...]
    y_ref[...] = b_ref[...]
    z_ref[...] = c_ref[...]


def settle(out, dx, gr):
    length, channels = out.shape
    width = min(1024, channels)
    specs = (
        pl.BlockSpec((length, width), lambda i: (0, i)),
        pl.BlockSpec((3, length, width), lambda i: (0, 0, i)),
        pl.BlockSpec(gr.shape, lambda i: (0, 0)),
    )
    return pl.pallas_call(
        pass_on,
        grid=(channels // width,),
        out_shape=tuple(jax.ShapeDtypeStruct(a.shape, a.dtype) for a in (out, dx, gr)),
        in_specs=list(specs),
        out_specs=specs,
        compiler_params=pltpu.CompilerParams(vmem_limit_bytes=16 * 1024 * 1024),
    )(out, dx, gr)


def on_device(n, qkv, g_out, residue, decay):
    length, _, channels = qkv.shape
    nb = channels // LANES
    per_chunk = 2
    nc = nb // per_chunk
    wide = jax.ShapeDtypeStruct((length, channels), bf16)
    vm = pl.BlockSpec(memory_space=pltpu.VMEM)
    dma = pltpu.SemaphoreType.DMA
    out, dx, gr = pl.pallas_call(
        functools.partial(kernel, n, nb, per_chunk, length),
        out_shape=(
            wide,
            jax.ShapeDtypeStruct((3, length, channels), bf16),
            jax.ShapeDtypeStruct((ORDER, nb * PER), f32),
        ),
        in_specs=[pl.BlockSpec(memory_space=pltpu.HBM)] * 2 + [vm] * 2,
        out_specs=(vm,) * 3,
        scratch_shapes=[
            pltpu.VMEM((length, channels), bf16),
            pltpu.VMEM((length, channels), bf16),
            pltpu.VMEM((length, channels), f32),
            pltpu.VMEM((length, channels), f32),
            pltpu.VMEM((length, channels), f32),
            pltpu.VMEM((length, channels), f32),
            pltpu.VMEM((nb, 2, ORDER, LANES), f32),
            pltpu.VMEM((nb, 2, ORDER, LANES), f32),
            pltpu.VMEM((nb, ORDER, LANES), f32),
            pltpu.VMEM((nb, ORDER, LANES), f32),
            pltpu.VMEM((nb, ORDER, LANES), f32),
            pltpu.VMEM((nb, ORDER, LANES), f32),
            pltpu.VMEM((PER, length), f32),
            pltpu.VMEM((ORDER, nb * PER), f32),
            pltpu.VMEM((n, ORDER, nb * PER), f32),
            pltpu.VMEM((nb, ORDER, LANES), f32),
            pltpu.VMEM((nb, 1, LANES), f32),
            pltpu.VMEM((nb, 1, LANES), f32),
            pltpu.VMEM((nb, 1, LANES), f32),
            pltpu.VMEM((2, 8 * length, LANES), bf16),
            pltpu.VMEM((8 * length, LANES), bf16),
            pltpu.VMEM((3, length, channels), bf16),
            pltpu.VMEM((length, channels), bf16),
            dma((nc,)), dma((nc,)), dma((nc,)), dma((nc,)), dma((nc,)), dma((nc,)),
            dma((n,)), dma((n,)), dma((nc,)), dma((nc,)),
        ],
        compiler_params=pltpu.CompilerParams(
            collective_id=0, has_side_effects=True, vmem_limit_bytes=40 * 1024 * 1024),
    )(jnp.transpose(qkv, (1, 0, 2)), g_out, decay.T, residue.T)
    out, dx, gr = settle(out, dx, gr)
    return out, jnp.transpose(dx, (1, 0, 2)), gr.T


def solution(mesh):
    return jax.shard_map(
        functools.partial(on_device, mesh.shape["ctx"]),
        mesh=mesh,
        in_specs=(
            P(("grp", "ctx"), None, "ch"),
            P(("grp", "ctx"), "ch"),
            P("ch", None),
            P("ch", None),
        ),
        out_specs=(P(("grp", "ctx"), "ch"), P(("grp", "ctx"), None, "ch"), P(("grp", "ch"), None)),
        check_vma=False,
    )
```

```python
import functools
import jax
import jax.numpy as jnp
from jax import lax
from jax.experimental import pallas as pl
from jax.experimental.pallas import tpu as pltpu
from jax.sharding import PartitionSpec as P

GROUP = 16
ORDER = 16
LANES = 256
PER = LANES // GROUP
ROWS = PER * ORDER
bf16 = jnp.bfloat16
f32 = jnp.float32
PAIR = 2
LEAD = 1
SLACK = 3


def split(a):
    hi = a.astype(bf16)
    return hi, (a - hi.astype(f32)).astype(bf16)


def mm(a, b, ca=1, cb=0):
    return lax.dot_general(a, b, (((ca,), (cb,)), ((), ())), preferred_element_type=f32)


def mm3(a, b, ca=1, cb=0):
    ah, al = split(a)
    bh, bl = split(b)
    return mm(ah, bh, ca, cb) + (mm(ah, bl, ca, cb) + mm(al, bh, ca, cb))


def iota(shape, dim):
    return lax.broadcasted_iota(jnp.int32, shape, dim)


def kernel(
    n, nb, per_chunk, length,
    x_hbm, g_hbm, dt_ref, rt_ref,
    out_ref, dx_ref, gr_ref,
    sig, cot, w0, w1, mix, gsig, own, peer, zf_in, zf_out, zb_in, zb_out, lags, gr_own, gr_all, drep, d_row, r_row, own_row, tmat, pmat, x_ref, g_ref,
    xs, xr, fs, fr, bs, br, gs, grs, xin, gin,
):
    me = lax.axis_index("ctx")
    side = lax.rem(me, PAIR)
    z = me // PAIR
    nz = n // PAIR
    nc = nb // per_chunk
    partner = me + 1 - 2 * side
    half = 128

    def load(i):
        cols = pl.ds(pl.multiple_of(i * per_chunk * LANES, LANES), per_chunk * LANES)
        return (
            pltpu.make_async_copy(x_hbm.at[:, :, cols], x_ref.at[:, :, cols], xin.at[i]),
            pltpu.make_async_copy(g_hbm.at[:, cols], g_ref.at[:, cols], gin.at[i]),
        )

    def load_start(i, c):
        for copy in load(i):
            copy.start()
        return c

    lax.fori_loop(0, nc, load_start, 0)
    barrier = pltpu.get_barrier_semaphore()

    def greet(i, c):
        pl.semaphore_signal(barrier, inc=1, device_id={"ctx": lax.rem(me + i, n)}, device_id_type=pl.DeviceIdType.MESH)
        return c

    lax.fori_loop(1, n, greet, 0)

    diag = (iota((ROWS, LANES), 0) // ORDER) == (iota((ROWS, LANES), 1) // GROUP)

    def chosen(j):
        groups = nb * PER
        hit = iota((groups, LANES), 0) == j * PER + iota((groups, LANES), 1) // GROUP
        return jnp.where(hit, 1.0, 0.0).astype(bf16)

    def spread(table, j):
        hi = table.astype(bf16)
        rest = table - hi.astype(f32)
        mid = rest.astype(bf16)
        low = (rest - mid.astype(f32)).astype(bf16)
        hot = chosen(j)
        return mm(hi, hot) + mm(mid, hot) + mm(low, hot)

    def states(j, c):
        cols = pl.ds(pl.multiple_of(j * LANES, LANES), LANES)
        sg = (x_ref[1, :, cols].astype(f32) * x_ref[2, :, cols].astype(f32)).astype(bf16)
        ct = (g_ref[:, cols].astype(f32) * x_ref[0, :, cols].astype(f32)).astype(bf16)
        sig[:, cols] = sg
        cot[:, cols] = ct
        wide = spread(dt_ref[...], j)
        own_mode = lax.rem(iota((ORDER, LANES), 1), ORDER) == iota((ORDER, LANES), 0)
        drep[j] = jnp.exp(-wide * float(length))
        d = jnp.sum(jnp.where(own_mode, wide, 0.0), axis=0, keepdims=True)
        d_row[j] = d
        r_row[j] = jnp.sum(jnp.where(own_mode, spread(rt_ref[...], j), 0.0), axis=0, keepdims=True)
        t = iota((length, LANES), 0).astype(f32)
        a0 = jnp.exp(-d * t)
        a1 = jnp.exp(-d * (length - t))
        w0[:, cols] = a0
        w1[:, cols] = a1
        for which, (a, x) in enumerate(((a1, sg), (a0, ct))):
            hi, lo = split(a.T)
            full = mm(hi, x) + mm(lo, x)
            own[j, which] = jnp.sum(jnp.where(diag, full, 0.0).reshape(PER, ORDER, LANES), axis=0)
        return c

    def xcopy(i):
        rows = pl.ds(i * per_chunk, per_chunk)
        return pltpu.make_async_remote_copy(
            src_ref=own.at[rows], dst_ref=peer.at[rows], send_sem=xs.at[i], recv_sem=xr.at[i],
            device_id={"ctx": partner}, device_id_type=pl.DeviceIdType.MESH)

    def zcopy(i, up):
        rows = pl.ds(i * per_chunk, per_chunk)
        src, dst, s, r = (zf_out, zf_in, fs, fr) if up else (zb_out, zb_in, bs, br)
        to = lax.rem(me + PAIR, n) if up else lax.rem(me + n - PAIR, n)
        return pltpu.make_async_remote_copy(
            src_ref=src.at[rows], dst_ref=dst.at[rows], send_sem=s.at[i], recv_sem=r.at[i],
            device_id={"ctx": to}, device_id_type=pl.DeviceIdType.MESH)

    def first(i, c):
        ahead(i, 0)
        xcopy(i).start()
        return c

    def ahead(i, c):
        for copy in load(i):
            copy.wait()
        for u in range(per_chunk):
            states(i * per_chunk + u, 0)
        return c

    early = nc // 2

    def send(i, c):
        xcopy(i).start()
        return c

    lax.fori_loop(0, early, ahead, 0)
    pl.semaphore_wait(barrier, n - 1)
    lax.fori_loop(0, early, send, 0)
    lax.fori_loop(early, nc, first, 0)

    def fade(j):
        return drep[j]

    lower = iota((length, length), 1) <= iota((length, length), 0)
    upper = iota((length, length), 1) >= iota((length, length), 0)
    across = iota((length, length), 0) + iota((length, length), 1)
    corner = across <= length - 1
    flip = jnp.where(across == length - 1, 1.0, 0.0).astype(bf16)
    pick = (iota((PER, ROWS), 1) // ORDER) == iota((PER, ROWS), 0)
    pick16 = jnp.where(pick, 1.0, 0.0).astype(bf16)

    def heavy(j):
        cols = pl.ds(pl.multiple_of(j * LANES, LANES), LANES)
        r = r_row[j]
        a0 = w0[:, cols]
        a1 = w1[:, cols]
        row0 = iota((length, LANES), 0) == 0
        h0, l0 = split(r * a0)
        h1, l1 = split(r * jnp.where(row0, 1.0, a1))
        h = mm(pick16, h0, 1, 1) + mm(pick16, l0, 1, 1)
        hr = mm(pick16, h1, 1, 1) + mm(pick16, l1, 1, 1)
        blank = jnp.zeros((length, half), bf16)

        def corners(a, b):
            return jnp.concatenate(
                [jnp.concatenate([a, blank], 1), jnp.concatenate([blank, b], 1)], 0)

        sgw = sig[:, cols]
        ctw = cot[:, cols]
        back = mm(flip, ctw).astype(bf16)
        per_half = half // GROUP
        lane_group = iota((length, half), 1) // GROUP
        for e in range(per_half):
            keep = lax.rem(iota((1, LANES), 1) // GROUP, per_half) == e
            pmat[pl.ds(e * length, length)] = back * jnp.where(keep, 1.0, 0.0).astype(bf16)
        pall = mm(pmat[...], corners(sgw[:, :half], sgw[:, half:]), 1, 1)
        for p in range(LANES // half):
            hc = pl.ds(pl.multiple_of(j * LANES + p * half, half), half)
            side_cols = slice(p * half, (p + 1) * half)
            for e in range(per_half):
                g = p * per_half + e
                rows = pl.ds(e * length, length)
                tt = pltpu.roll(jnp.broadcast_to(h[g:g + 1], (length, length)), 0, 1, stride=1, stride_axis=0)
                tmat[p, rows, half:] = jnp.where(upper, tt, 0.0).astype(bf16)
                tf = pltpu.roll(jnp.broadcast_to(hr[g:g + 1], (length, length)), 0, 1, stride=1, stride_axis=0)
                tmat[p, rows, :half] = jnp.where(lower, tf, 0.0).astype(bf16)
            both = mm(tmat[p], corners(sgw[:, side_cols], ctw[:, side_cols]))
            macc = both[:length, :half]
            gacc = both[:length, half:]
            for e in range(per_half):
                g = p * per_half + e
                at = slice(e * length, (e + 1) * length)
                if e:
                    macc = jnp.where(lane_group == e, both[at, :half], macc)
                    gacc = jnp.where(lane_group == e, both[at, half:], gacc)
                m = pltpu.roll(jnp.where(corner, pall[at, side_cols], 0.0), 0, 1, stride=1, stride_axis=0)
                lags[g:g + 1, :] = jnp.sum(m, axis=0, keepdims=True)
            mix[:, hc] = macc
            gsig[:, hc] = gacc
        full = mm3(lags[...], jnp.exp(-d_row[j] * (length - 1 - iota((length, LANES), 0)).astype(f32)))
        own_row[j] = jnp.sum(jnp.where(pick, full, 0.0), axis=0, keepdims=True)

    steps = max(nb, LEAD + nc + SLACK * (nz - 1))

    def comm(step):
        i = step - SLACK * z

        @pl.when((i >= 0) & (i < nc))
        def _():
            @pl.when(z > 0)
            def _():
                zcopy(i, True).wait_recv()

            @pl.when(z < nz - 1)
            def _():
                for u in range(per_chunk):
                    j = i * per_chunk + u
                    f = fade(j)
                    mine, other = own[j, 0], peer[j, 0]
                    pair = jnp.where(side == 0, f * mine + other, f * other + mine)
                    zf_out[j] = pair + jnp.where(z > 0, f * f * zf_in[j], 0.0)
                zcopy(i, True).start()

        i2 = step - SLACK * (nz - 1 - z)

        @pl.when((i2 >= 0) & (i2 < nc))
        def _():
            @pl.when(z < nz - 1)
            def _():
                zcopy(i2, False).wait_recv()

            @pl.when(z > 0)
            def _():
                for u in range(per_chunk):
                    j = i2 * per_chunk + u
                    f = fade(j)
                    mine, other = own[j, 1], peer[j, 1]
                    pair = jnp.where(side == 0, mine + f * other, other + f * mine)
                    zb_out[j] = pair + jnp.where(z < nz - 1, f * f * zb_in[j], 0.0)
                zcopy(i2, False).start()

    @pl.when(z == 0)
    def _():
        zf_in[...] = jnp.zeros_like(zf_in)

    @pl.when(z == nz - 1)
    def _():
        zb_in[...] = jnp.zeros_like(zb_in)

    def second(s, c):
        @pl.when(s < nb)
        def _():
            heavy(s)

        @pl.when((s >= LEAD) & (s - LEAD < nc))
        def _():
            xcopy(s - LEAD).wait_recv()

        @pl.when(s >= LEAD)
        def _():
            comm(s - LEAD)

        return c

    lax.fori_loop(0, steps, second, 0)

    def carries(j, acc):
        f = fade(j)
        zf, zb = zf_in[j], zb_in[j]
        cf = jnp.where(side == 0, zf, f * zf + peer[j, 0])
        cb = jnp.where(side == 0, f * zb + peer[j, 1], zb)
        zf_in[j] = cf
        zb_in[j] = cb
        own_mode = lax.rem(iota((ORDER, LANES), 1), ORDER) == iota((ORDER, LANES), 0)
        hi, lo = split(own[j, 1] * cf + jnp.where(own_mode, own_row[j], 0.0))
        hot = chosen(j)
        return acc + mm(hi, hot, 1, 1) + mm(lo, hot, 1, 1)

    gr_own[...] = lax.fori_loop(0, nb, carries, jnp.zeros(gr_own.shape, f32), unroll=4)

    def gcopy(i):
        to = lax.rem(me + i, n)
        return pltpu.make_async_remote_copy(
            src_ref=gr_own, dst_ref=gr_all.at[i], send_sem=gs.at[i], recv_sem=grs.at[i],
            device_id={"ctx": to}, device_id_type=pl.DeviceIdType.MESH)

    def gstart(i, c):
        gcopy(i).start()
        return c

    lax.fori_loop(1, n, gstart, 0)

    def last(j, c):
        cols = pl.ds(pl.multiple_of(j * LANES, LANES), LANES)
        r = r_row[j]
        cf = jnp.where(diag, jnp.concatenate([zf_in[j]] * PER, 0), 0.0)
        cb = jnp.where(diag, jnp.concatenate([zb_in[j]] * PER, 0), 0.0)
        m = mix[:, cols] + mm3(r * w0[:, cols], cf)
        gsv = gsig[:, cols] + mm3(r * w1[:, cols], cb)
        out_ref[:, cols] = (x_ref[0, :, cols].astype(f32) * m).astype(bf16)
        dx_ref[0, :, cols] = (g_ref[:, cols].astype(f32) * m).astype(bf16)
        dx_ref[1, :, cols] = (gsv * x_ref[2, :, cols].astype(f32)).astype(bf16)
        dx_ref[2, :, cols] = (gsv * x_ref[1, :, cols].astype(f32)).astype(bf16)
        return c

    lax.fori_loop(0, nb, last, 0, unroll=2)

    def xend(i, c):
        xcopy(i).wait_send()

        @pl.when(z < nz - 1)
        def _():
            zcopy(i, True).wait_send()

        @pl.when(z > 0)
        def _():
            zcopy(i, False).wait_send()

        return c

    lax.fori_loop(0, nc, xend, 0)

    def gend(i, c):
        gcopy(i).wait()
        return c

    lax.fori_loop(1, n, gend, 0)

    def gsum(i, acc):
        return acc + gr_all[i]

    gr_ref[...] = lax.fori_loop(1, n, gsum, gr_own[...])


def pass_on(a_ref, b_ref, c_ref, x_ref, y_ref, z_ref):
    x_ref[...] = a_ref[...]
    y_ref[...] = b_ref[...]
    z_ref[...] = c_ref[...]


def settle(out, dx, gr):
    length, channels = out.shape
    width = min(2048, channels)
    specs = (
        pl.BlockSpec((length, width), lambda i: (0, i)),
        pl.BlockSpec((3, length, width), lambda i: (0, 0, i)),
        pl.BlockSpec(gr.shape, lambda i: (0, 0)),
    )
    return pl.pallas_call(
        pass_on,
        grid=(channels // width,),
        out_shape=tuple(jax.ShapeDtypeStruct(a.shape, a.dtype) for a in (out, dx, gr)),
        in_specs=list(specs),
        out_specs=specs,
        compiler_params=pltpu.CompilerParams(vmem_limit_bytes=16 * 1024 * 1024),
    )(out, dx, gr)


def on_device(n, qkv, g_out, residue, decay):
    length, _, channels = qkv.shape
    nb = channels // LANES
    per_chunk = 2
    nc = nb // per_chunk
    wide = jax.ShapeDtypeStruct((length, channels), bf16)
    vm = pl.BlockSpec(memory_space=pltpu.VMEM)
    dma = pltpu.SemaphoreType.DMA
    out, dx, gr = pl.pallas_call(
        functools.partial(kernel, n, nb, per_chunk, length),
        out_shape=(
            wide,
            jax.ShapeDtypeStruct((3, length, channels), bf16),
            jax.ShapeDtypeStruct((ORDER, nb * PER), f32),
        ),
        in_specs=[pl.BlockSpec(memory_space=pltpu.HBM)] * 2 + [vm] * 2,
        out_specs=(vm,) * 3,
        scratch_shapes=[
            pltpu.VMEM((length, channels), bf16),
            pltpu.VMEM((length, channels), bf16),
            pltpu.VMEM((length, channels), f32),
            pltpu.VMEM((length, channels), f32),
            pltpu.VMEM((length, channels), f32),
            pltpu.VMEM((length, channels), f32),
            pltpu.VMEM((nb, 2, ORDER, LANES), f32),
            pltpu.VMEM((nb, 2, ORDER, LANES), f32),
            pltpu.VMEM((nb, ORDER, LANES), f32),
            pltpu.VMEM((nb, ORDER, LANES), f32),
            pltpu.VMEM((nb, ORDER, LANES), f32),
            pltpu.VMEM((nb, ORDER, LANES), f32),
            pltpu.VMEM((PER, length), f32),
            pltpu.VMEM((ORDER, nb * PER), f32),
            pltpu.VMEM((n, ORDER, nb * PER), f32),
            pltpu.VMEM((nb, ORDER, LANES), f32),
            pltpu.VMEM((nb, 1, LANES), f32),
            pltpu.VMEM((nb, 1, LANES), f32),
            pltpu.VMEM((nb, 1, LANES), f32),
            pltpu.VMEM((2, 8 * length, LANES), bf16),
            pltpu.VMEM((8 * length, LANES), bf16),
            pltpu.VMEM((3, length, channels), bf16),
            pltpu.VMEM((length, channels), bf16),
            dma((nc,)), dma((nc,)), dma((nc,)), dma((nc,)), dma((nc,)), dma((nc,)),
            dma((n,)), dma((n,)), dma((nc,)), dma((nc,)),
        ],
        compiler_params=pltpu.CompilerParams(
            collective_id=0, has_side_effects=True, vmem_limit_bytes=40 * 1024 * 1024),
    )(jnp.transpose(qkv, (1, 0, 2)), g_out, decay.T, residue.T)
    out, dx, gr = settle(out, dx, gr)
    return out, jnp.transpose(dx, (1, 0, 2)), gr.T


def solution(mesh):
    return jax.shard_map(
        functools.partial(on_device, mesh.shape["ctx"]),
        mesh=mesh,
        in_specs=(
            P(("grp", "ctx"), None, "ch"),
            P(("grp", "ctx"), "ch"),
            P("ch", None),
            P("ch", None),
        ),
        out_specs=(P(("grp", "ctx"), "ch"), P(("grp", "ctx"), None, "ch"), P(("grp", "ch"), None)),
        check_vma=False,
    )
```
